32 devices in a mesh: groups: 2 (over y), rows: 16 (over z, x, core).
Axes of the slice: x: 2, y: 2, z: 4, core: 2. Of those that a mesh axis runs over, the one named last changes fastest.
Arguments:
- latent: bfloat16 [64, 256, 512], P(('groups', 'rows')), parts along dimension 0, may hold values from -100 to 100
- gain_in: float32 [512], replicated, may hold values from 0.1 to 1.9
- shift_in: float32 [512], replicated, may hold values from -3 to 3
- conv_in: bfloat16 [4608, 256], replicated, may hold values from -0.09375 to 0.09375
- gain_mid: float32 [256], replicated, may hold values from 0.1 to 1.9
- shift_mid: float32 [256], replicated, may hold values from -3 to 3
- conv_mid: bfloat16 [2304, 256], replicated, may hold values from -0.125 to 0.125
- skip_weight: bfloat16 [512, 256], replicated, may hold values from -0.25 to 0.25
Outputs:
- decoded: bfloat16 [128, 512, 256], P(('groups', 'rows')), parts along dimension 0
The draws below stay inside these ranges and needn't reach their ends.
There are 2 independent parts, one for each index of `groups`. The reference program is written for one: setup_inputs(seed, part) draws one part's arguments, and reference() takes and returns one part's arrays. A program takes and returns all parts, laid end to end along the dimension named above; an argument that names none is the same for every part. Nothing has to cross between parts.
All inputs are finite; a program needn't handle non-finite values.
Results may differ from the reference program's by a relative error of at most 0.009.
Values may be sent and summed in bfloat16 or wider, within the bound.
A program may use at most 64 MiB of HBM per device.

```python
import math
import jax
import jax.numpy as jnp
from jax import lax

C_IN = 512
C_OUT = 256
GROUPS = 32
R_IN = 2
W_IN = 256
H_IN = 32


def draw_latent(key, part):
    subkeys = jax.random.split(key, 4)
    noise = jnp.clip(jax.random.normal(subkeys[0], (H_IN, W_IN, C_IN), jnp.float32), -4.0, 4.0)
    position = jnp.arange(H_IN, dtype=jnp.float32) / max(H_IN - 1, 1)
    row_scale = jnp.exp(position * math.log(3.0) + jax.random.uniform(subkeys[1], (H_IN,), jnp.float32, 0.0, math.log(3.3)))
    band_parity = (jnp.arange(H_IN, dtype=jnp.int32) // R_IN % 2).astype(jnp.float32)
    row_scale = row_scale * (1.0 - 0.75 * band_parity)
    col_scale = jnp.exp(jax.random.uniform(subkeys[2], (W_IN,), jnp.float32, 0.0, math.log(10.0)))
    chan_scale = jnp.exp(jax.random.uniform(subkeys[3], (C_IN,), jnp.float32, math.log(0.5), math.log(2.0)))
    value = 0.1 * noise * row_scale[:, None, None] * col_scale[None, :, None] * chan_scale[None, None, :]
    return value.astype(jnp.bfloat16)


def normal_values(stream_key, dims, scale, reach, kind=jnp.bfloat16):
    values = scale * jax.random.normal(stream_key, dims, jnp.float32)
    return jnp.clip(values, min=-reach, max=reach).astype(kind)


def setup_inputs(seed: int = 0, part: int = 0) -> dict:
    splits = jax.random.split(jax.random.key(seed), 9)
    part_splits = jax.random.split(jax.random.fold_in(splits[8], part), 9)
    latent = draw_latent(jax.random.fold_in(jax.random.fold_in(splits[8], part), 71), part)
    gain_in = jnp.clip(1.0 + 0.18 * jax.random.normal(splits[1], (C_IN,), jnp.float32), 0.1, 1.9)
    shift_in = normal_values(splits[2], (C_IN,), 0.5, 3.0, jnp.float32)
    conv_in = normal_values(splits[3], (9 * C_IN, C_OUT), (9 * C_IN) ** -0.5, 0.09375)
    gain_mid = jnp.clip(1.0 + 0.18 * jax.random.normal(splits[4], (C_OUT,), jnp.float32), 0.1, 1.9)
    shift_mid = normal_values(splits[5], (C_OUT,), 0.5, 3.0, jnp.float32)
    conv_mid = normal_values(splits[6], (9 * C_OUT, C_OUT), (9 * C_OUT) ** -0.5, 0.125)
    skip_weight = normal_values(splits[7], (C_IN, C_OUT), C_IN ** -0.5, 0.25)
    return dict(latent=latent, gain_in=gain_in, shift_in=shift_in, conv_in=conv_in, gain_mid=gain_mid, shift_mid=shift_mid, conv_mid=conv_mid, skip_weight=skip_weight)


def group_norm(values, gain, shift):
    height, breadth, chans = values.shape
    grouped = values.reshape(height * breadth, GROUPS, chans // GROUPS)
    center = lax.optimization_barrier(jnp.mean(grouped, axis=(0, 2)))
    deviate = grouped - center[None, :, None]
    spread = lax.optimization_barrier(jnp.mean(deviate * deviate, axis=(0, 2)))
    normed = deviate / jnp.sqrt(spread[None, :, None] + 1e-06)
    return normed.reshape(height, breadth, chans) * gain + shift

def convolve(values, weight):
    height, breadth, chans = values.shape
    padded = jnp.pad(values, ((1, 1), (1, 1), (0, 0)))
    accum = jnp.zeros((height * breadth, weight.shape[1]), jnp.float32)
    for offset_index in range(9):
        shift_row = offset_index // 3
        shift_col = offset_index % 3
        window = padded[shift_row:shift_row + height, shift_col:shift_col + breadth].reshape(-1, chans)
        accum = accum + jnp.dot(window, weight[offset_index * chans:(offset_index + 1) * chans], preferred_element_type=jnp.float32)
    return accum.reshape(height, breadth, -1)

def reference(latent, gain_in, shift_in, conv_in, gain_mid, shift_mid, conv_mid, skip_weight):
    act = jax.nn.silu(group_norm(latent.astype(jnp.float32), gain_in, shift_in)).astype(jnp.bfloat16)
    upsampled = jnp.repeat(jnp.repeat(act, 2, axis=0), 2, axis=1)
    hidden = convolve(upsampled, conv_in).astype(jnp.bfloat16)
    middle = jax.nn.silu(group_norm(hidden.astype(jnp.float32), gain_mid, shift_mid)).astype(jnp.bfloat16)
    height, breadth, chans = upsampled.shape
    skipped = jnp.dot(upsampled.reshape(-1, chans), skip_weight, preferred_element_type=jnp.float32).reshape(height, breadth, -1)
    return (convolve(middle, conv_mid) + skipped).astype(jnp.bfloat16)
```

```python
import functools

import jax
import jax.numpy as jnp
from jax import lax
from jax.experimental import pallas as pl
from jax.experimental.pallas import tpu as pltpu
from jax.sharding import PartitionSpec as P

GROUPS = 32
EPS = 1e-06
MESH = pl.DeviceIdType.MESH
F32 = jnp.float32
BF16 = jnp.bfloat16

TAP_ORDER = (0, 2, 6, 8, 1, 7, 3, 5, 4)


def dot(a, b):
    return jnp.dot(a, b, preferred_element_type=F32)


def group_total(x, width):
    lane = lax.broadcasted_iota(jnp.int32, x.shape, 1)
    step = 1
    while step < width:
        up = pltpu.roll(x, 128 - step, 1)
        down = pltpu.roll(x, step, 1)
        x = x + jnp.where((lane & step) == 0, up, down)
        step *= 2
    return x


def flat_row(x):
    return jnp.concatenate([x[k : k + 1] for k in range(x.shape[0])], axis=1)


def half_affine(total, width, count, gain, shift):
    rows = gain.shape[1] // 128
    total = group_total(total, width)
    mean = total[0:rows] / count
    var = jnp.maximum(total[rows : 2 * rows] / count - mean * mean, 0.0)
    inv = flat_row(lax.rsqrt(var + EPS))
    mean = flat_row(mean)
    scale = gain * inv
    return 0.5 * scale, 0.5 * (shift - mean * scale)


def silu_of_half(u):
    return u + u * jnp.tanh(u)


def kernel(
    n,
    latent,
    gain_in,
    shift_in,
    conv_in,
    gain_mid,
    shift_mid,
    conv_mid,
    skip_w,
    out,
    xraw,
    xcat,
    w1,
    w2,
    ws,
    de,
    be,
    df,
    bf,
    hid,
    mid,
    skip,
    inter,
    stage,
    stat,
    slots1,
    slots2,
    local_sem,
    halo_send,
    halo_recv,
    stat_send,
    stat_recv,
    out_sem,
):
    me = lax.axis_index("rows")
    width = latent.shape[1]
    chans = latent.shape[2]
    pad = xcat.shape[1]
    outs = out.shape[2]
    first = me == 0
    last = me == n - 1

    load_x = pltpu.make_async_copy(latent, xraw.at[pl.ds(1, 2)], local_sem.at[0])
    load_x.start()
    barrier = pltpu.get_barrier_semaphore()

    def greet(d, carry):
        pl.semaphore_signal(
            barrier, inc=1, device_id={"rows": lax.rem(me + d, n)}, device_id_type=MESH
        )
        return carry

    lax.fori_loop(1, n, greet, 0)
    loads = []
    for slot, tap in enumerate(TAP_ORDER):
        loads.append(
            pltpu.make_async_copy(
                conv_in.at[pl.ds(tap * chans, chans)],
                w1.at[pl.ds(slot * chans, chans)],
                local_sem.at[1 + slot],
            )
        )
    load_w2 = pltpu.make_async_copy(conv_mid, w2, local_sem.at[10])
    load_ws = pltpu.make_async_copy(skip_w, ws, local_sem.at[11])
    for c in loads + [load_ws, load_w2]:
        c.start()

    def peer_copy(slots, index, d):
        return pltpu.make_async_remote_copy(
            src_ref=stat.at[index],
            dst_ref=slots.at[d - 1],
            send_sem=stat_send.at[index, d - 1],
            recv_sem=stat_recv.at[index, d - 1],
            device_id={"rows": lax.rem(me + d, n)},
            device_id_type=MESH,
        )

    def exchange(slots, index):
        def send(d, carry):
            peer_copy(slots, index, d).start()
            return carry

        lax.fori_loop(1, n, send, 0)

    def gathered(slots, index):
        def receive(d, carry):
            peer_copy(slots, index, d).wait_recv()
            return carry

        lax.fori_loop(1, n, receive, 0)
        return stat[index] + jnp.sum(slots[...], axis=0)

    load_x.wait()
    x = xraw[1:3].reshape(2 * width, chans).astype(F32)
    total = jnp.sum(x, axis=0, keepdims=True)
    square = jnp.sum(x * x, axis=0, keepdims=True)
    lanes = chans // 128
    for k in range(lanes):
        stat[0, k : k + 1, :] = total[:, 128 * k : 128 * (k + 1)]
        stat[0, lanes + k : lanes + k + 1, :] = square[:, 128 * k : 128 * (k + 1)]

    pl.semaphore_wait(barrier, n - 1)
    exchange(slots1, 0)
    to_next = pltpu.make_async_remote_copy(
        src_ref=xraw.at[2],
        dst_ref=xraw.at[0],
        send_sem=halo_send.at[0],
        recv_sem=halo_recv.at[0],
        device_id={"rows": lax.rem(me + 1, n)},
        device_id_type=MESH,
    )
    to_prev = pltpu.make_async_remote_copy(
        src_ref=xraw.at[1],
        dst_ref=xraw.at[3],
        send_sem=halo_send.at[1],
        recv_sem=halo_recv.at[1],
        device_id={"rows": lax.rem(me + n - 1, n)},
        device_id_type=MESH,
    )

    @pl.when(jnp.logical_not(last))
    def _():
        to_next.start()

    @pl.when(jnp.logical_not(first))
    def _():
        to_prev.start()

    count1 = float(2 * n * width * (chans // GROUPS))
    scale1, bias1 = half_affine(
        gathered(slots1, 0), chans // GROUPS, count1, gain_in[...], shift_in[...]
    )

    row_in = lax.broadcasted_iota(jnp.int32, (width, chans), 0)
    tail_in = lax.broadcasted_iota(jnp.int32, (8, chans), 0)
    zeros_tail = jnp.zeros((pad - width, chans), BF16)

    def activate(i):
        y = silu_of_half(xraw[i].astype(F32) * scale1 + bias1)
        turned = pltpu.roll(y, 1, 0)
        xcat[i, 0:width, 0:chans] = jnp.where(row_in == 0, 0.0, turned).astype(BF16)
        end = jnp.where(tail_in == 0, turned[0:8], 0.0)
        end = jnp.concatenate([end, jnp.zeros((pad - width - 8, chans), F32)], axis=0)
        xcat[i, width:pad, 0:chans] = end.astype(BF16)
        xcat[i, 0:width, chans:] = y.astype(BF16)
        xcat[i, width:pad, chans:] = zeros_tail

    activate(1)
    activate(2)
    for c in loads:
        c.wait()

    def products(ks, bs):
        pairs = [jnp.concatenate([xcat[k], xcat[k + 1]], axis=1) for k in ks]
        res = dot(jnp.concatenate(pairs, axis=0), w1[0 : 4 * chans])
        for p, k in enumerate(ks):
            de[k] = res[p * pad : (p + 1) * pad]
        pairs = [
            jnp.concatenate([xcat[k, 0:width, chans:], xcat[k + 1, 0:width, chans:]], axis=1)
            for k in ks
        ]
        res = dot(jnp.concatenate(pairs, axis=0), w1[4 * chans : 6 * chans])
        for p, k in enumerate(ks):
            df[k] = res[p * width : (p + 1) * width]
        res = dot(jnp.concatenate([xcat[i] for i in bs], axis=0), w1[6 * chans : 8 * chans])
        for p, i in enumerate(bs):
            be[i] = res[p * pad : (p + 1) * pad]
        res = dot(jnp.concatenate([xcat[i, 0:width, chans:] for i in bs], axis=0), w1[8 * chans : 9 * chans])
        for p, i in enumerate(bs):
            bf[i] = res[p * width : (p + 1) * width]

    sums = [jnp.zeros((8, outs), F32), jnp.zeros((8, outs), F32)]

    def combine(r):
        k, i = r // 2, (r + 1) // 2
        edge = de[k] + be[i]
        whole = df[k] + bf[i]
        even = edge[0:width] + whole
        odd = pltpu.roll(edge, pad - 1, 0)[0:width] + whole
        hid[r, :, 0:outs] = even.astype(BF16)
        hid[r, :, outs:] = odd.astype(BF16)
        if 1 <= r <= 4:
            for v in (even, odd):
                v = v.reshape(width // 8, 8, outs)
                sums[0] = sums[0] + jnp.sum(v, axis=0)
                sums[1] = sums[1] + jnp.sum(v * v, axis=0)

    products((1,), (1, 2))
    combine(2)
    combine(3)

    @pl.when(jnp.logical_not(first))
    def _():
        to_next.wait_recv()
        activate(0)

    @pl.when(first)
    def _():
        xcat[0] = jnp.zeros(xcat.shape[1:], BF16)

    @pl.when(jnp.logical_not(last))
    def _():
        to_prev.wait_recv()
        activate(3)

    @pl.when(last)
    def _():
        xcat[3] = jnp.zeros(xcat.shape[1:], BF16)

    products((0, 2), (0, 3))
    for r in (1, 4, 0, 5):
        combine(r)

    total = jnp.sum(sums[0], axis=0, keepdims=True)
    square = jnp.sum(sums[1], axis=0, keepdims=True)
    lanes = outs // 128
    stat[1] = jnp.zeros(stat.shape[1:], F32)
    for k in range(lanes):
        stat[1, k : k + 1, :] = total[:, 128 * k : 128 * (k + 1)]
        stat[1, lanes + k : lanes + k + 1, :] = square[:, 128 * k : 128 * (k + 1)]
    exchange(slots2, 1)

    load_ws.wait()
    for i in range(2):
        skip[i] = dot(xcat[1 + i, 0:width, chans:], ws[...])
    load_w2.wait()

    count2 = float(8 * n * width * (outs // GROUPS))
    scale2, bias2 = half_affine(
        gathered(slots2, 1), outs // GROUPS, count2, gain_mid[...], shift_mid[...]
    )
    row_mid = lax.broadcasted_iota(jnp.int32, (width, outs), 0)

    def middle(r):
        even = silu_of_half(hid[r, :, 0:outs].astype(F32) * scale2 + bias2)
        odd = silu_of_half(hid[r, :, outs:].astype(F32) * scale2 + bias2)
        if r == 0:
            even = jnp.where(first, 0.0, even)
            odd = jnp.where(first, 0.0, odd)
        if r == 5:
            even = jnp.where(last, 0.0, even)
            odd = jnp.where(last, 0.0, odd)
        before = jnp.where(row_mid == 0, 0.0, pltpu.roll(odd, 1, 0))
        after = jnp.where(row_mid == width - 1, 0.0, pltpu.roll(even, width - 1, 0))
        mid[r, :, 0:outs] = before.astype(BF16)
        mid[r, :, outs : 2 * outs] = even.astype(BF16)
        mid[r, :, 2 * outs : 3 * outs] = odd.astype(BF16)
        mid[r, :, 3 * outs :] = after.astype(BF16)

    def second(pair):
        rows = (2 * pair, 2 * pair + 1)
        base = jnp.concatenate([skip[pair], skip[pair]], axis=0)
        for parity in range(2):
            cols = pl.ds(parity * outs, 3 * outs)
            lhs = jnp.concatenate(
                [
                    jnp.concatenate([mid[r + a, :, cols] for a in range(3)], axis=1)
                    for r in rows
                ],
                axis=0,
            )
            res = dot(lhs, w2[...]) + base
            for h in range(outs // 128):
                inter[pair, h, pl.ds(parity, 2 * width, stride=2), :] = res[
                    :, 128 * h : 128 * (h + 1)
                ]
        for h in range(outs // 128):
            stage[2 * pair : 2 * pair + 2, :, 128 * h : 128 * (h + 1)] = (
                inter[pair, h].astype(BF16).reshape(2, 2 * width, 128)
            )
        pltpu.make_async_copy(
            stage.at[pl.ds(2 * pair, 2)], out.at[pl.ds(2 * pair, 2)], out_sem.at[pair]
        ).start()

    for r in range(4):
        middle(r)
    second(0)
    middle(4)
    middle(5)
    second(1)

    for pair in range(2):
        pltpu.make_async_copy(
            stage.at[pl.ds(2 * pair, 2)], out.at[pl.ds(2 * pair, 2)], out_sem.at[pair]
        ).wait()
    for index, slots in enumerate((slots1, slots2)):

        def sent(d, carry):
            peer_copy(slots, index, d).wait_send()
            return carry

        lax.fori_loop(1, n, sent, 0)

    @pl.when(jnp.logical_not(last))
    def _():
        to_next.wait_send()

    @pl.when(jnp.logical_not(first))
    def _():
        to_prev.wait_send()


def body(n, latent, gain_in, shift_in, conv_in, gain_mid, shift_mid, conv_mid, skip_weight):
    rows, width, chans = latent.shape
    outs = skip_weight.shape[1]
    pad = width + 16
    anywhere = pl.BlockSpec(memory_space=pl.ANY)
    vmem = pl.BlockSpec(memory_space=pltpu.VMEM)
    return pl.pallas_call(
        functools.partial(kernel, n),
        out_shape=jax.ShapeDtypeStruct((2 * rows, 2 * width, outs), BF16),
        in_specs=[anywhere, vmem, vmem, anywhere, vmem, vmem, anywhere, anywhere],
        out_specs=anywhere,
        scratch_shapes=[
            pltpu.VMEM((4, width, chans), BF16),
            pltpu.VMEM((4, pad, 2 * chans), BF16),
            pltpu.VMEM((9 * chans, outs), BF16),
            pltpu.VMEM((9 * outs, outs), BF16),
            pltpu.VMEM((chans, outs), BF16),
            pltpu.VMEM((3, pad, outs), F32),
            pltpu.VMEM((4, pad, outs), F32),
            pltpu.VMEM((3, width, outs), F32),
            pltpu.VMEM((4, width, outs), F32),
            pltpu.VMEM((6, width, 2 * outs), BF16),
            pltpu.VMEM((6, width, 4 * outs), BF16),
            pltpu.VMEM((2, width, outs), F32),
            pltpu.VMEM((2, outs // 128, 4 * width, 128), F32),
            pltpu.VMEM((4, 2 * width, outs), BF16),
            pltpu.VMEM((2, 8, 128), F32),
            pltpu.VMEM((n - 1, 8, 128), F32),
            pltpu.VMEM((n - 1, 8, 128), F32),
            pltpu.SemaphoreType.DMA((12,)),
            pltpu.SemaphoreType.DMA((2,)),
            pltpu.SemaphoreType.DMA((2,)),
            pltpu.SemaphoreType.DMA((2, n - 1)),
            pltpu.SemaphoreType.DMA((2, n - 1)),
            pltpu.SemaphoreType.DMA((2,)),
        ],
        compiler_params=pltpu.CompilerParams(
            collective_id=0, has_side_effects=True, vmem_limit_bytes=56 * 1024 * 1024
        ),
        cost_estimate=pl.CostEstimate(
            flops=4_700_000_000, bytes_accessed=5_400_000, transcendentals=1_300_000
        ),
    )(
        latent,
        gain_in.reshape(1, chans),
        shift_in.reshape(1, chans),
        conv_in,
        gain_mid.reshape(1, outs),
        shift_mid.reshape(1, outs),
        conv_mid,
        skip_weight,
    )


def solution(mesh):
    placed = (P(("groups", "rows"), None, None), P(), P(), P(), P(), P(), P(), P())
    return jax.shard_map(
        functools.partial(body, mesh.shape["rows"]),
        mesh=mesh,
        in_specs=placed,
        out_specs=P(("groups", "rows"), None, None),
        check_vma=False,
    )
```

```python
import functools

import jax
import jax.numpy as jnp
from jax import lax
from jax.experimental import pallas as pl
from jax.experimental.pallas import tpu as pltpu
from jax.sharding import PartitionSpec as P

GROUPS = 32
EPS = 1e-06
MESH = pl.DeviceIdType.MESH
F32 = jnp.float32
BF16 = jnp.bfloat16

TAP_ORDER = (0, 2, 6, 8, 1, 7, 3, 5, 4)


def dot(a, b):
    return jnp.dot(a, b, preferred_element_type=F32)


def group_total(x, width):
    lane = lax.broadcasted_iota(jnp.int32, x.shape, 1)
    step = 1
    while step < width:
        up = pltpu.roll(x, 128 - step, 1)
        down = pltpu.roll(x, step, 1)
        x = x + jnp.where((lane & step) == 0, up, down)
        step *= 2
    return x


def flat_row(x):
    return jnp.concatenate([x[k : k + 1] for k in range(x.shape[0])], axis=1)


def half_affine(total, width, count, gain, shift):
    rows = gain.shape[1] // 128
    total = group_total(total, width)
    mean = total[0:rows] / count
    var = jnp.maximum(total[rows : 2 * rows] / count - mean * mean, 0.0)
    inv = flat_row(lax.rsqrt(var + EPS))
    mean = flat_row(mean)
    scale = gain * inv
    return 0.5 * scale, 0.5 * (shift - mean * scale)


def silu_of_half(u):
    return u + u * jnp.tanh(u)


def kernel(
    n,
    latent,
    gain_in,
    shift_in,
    conv_in,
    gain_mid,
    shift_mid,
    conv_mid,
    skip_w,
    out,
    xraw,
    xcat,
    w1,
    w2,
    ws,
    de,
    be,
    df,
    bf,
    hid,
    mid,
    skip,
    inter,
    stat,
    slots1,
    slots2,
    local_sem,
    halo_send,
    halo_recv,
    stat_send,
    stat_recv,
):
    me = lax.axis_index("rows")
    width = latent.shape[1]
    chans = latent.shape[2]
    pad = xcat.shape[1]
    outs = out.shape[2]
    first = me == 0
    last = me == n - 1

    load_x = pltpu.make_async_copy(latent, xraw.at[pl.ds(1, 2)], local_sem.at[0])
    load_x.start()
    barrier = pltpu.get_barrier_semaphore()

    def greet(d, carry):
        pl.semaphore_signal(
            barrier, inc=1, device_id={"rows": lax.rem(me + d, n)}, device_id_type=MESH
        )
        return carry

    lax.fori_loop(1, n, greet, 0)
    loads = []
    for slot, tap in enumerate(TAP_ORDER):
        loads.append(
            pltpu.make_async_copy(
                conv_in.at[pl.ds(tap * chans, chans)],
                w1.at[pl.ds(slot * chans, chans)],
                local_sem.at[1 + slot],
            )
        )
    load_w2 = pltpu.make_async_copy(conv_mid, w2, local_sem.at[10])
    load_ws = pltpu.make_async_copy(skip_w, ws, local_sem.at[11])
    for c in loads + [load_ws, load_w2]:
        c.start()

    def peer_copy(slots, index, d):
        return pltpu.make_async_remote_copy(
            src_ref=stat.at[index],
            dst_ref=slots.at[d - 1],
            send_sem=stat_send.at[index, d - 1],
            recv_sem=stat_recv.at[index, d - 1],
            device_id={"rows": lax.rem(me + d, n)},
            device_id_type=MESH,
        )

    def exchange(slots, index):
        def send(d, carry):
            peer_copy(slots, index, d).start()
            return carry

        lax.fori_loop(1, n, send, 0)

    def gathered(slots, index):
        def receive(d, carry):
            peer_copy(slots, index, d).wait_recv()
            return carry

        lax.fori_loop(1, n, receive, 0)
        return stat[index] + jnp.sum(slots[...], axis=0)

    load_x.wait()
    x = xraw[1:3].reshape(2 * width, chans).astype(F32)
    total = jnp.sum(x, axis=0, keepdims=True)
    square = jnp.sum(x * x, axis=0, keepdims=True)
    lanes = chans // 128
    for k in range(lanes):
        stat[0, k : k + 1, :] = total[:, 128 * k : 128 * (k + 1)]
        stat[0, lanes + k : lanes + k + 1, :] = square[:, 128 * k : 128 * (k + 1)]

    pl.semaphore_wait(barrier, n - 1)
    exchange(slots1, 0)
    to_next = pltpu.make_async_remote_copy(
        src_ref=xraw.at[2],
        dst_ref=xraw.at[0],
        send_sem=halo_send.at[0],
        recv_sem=halo_recv.at[0],
        device_id={"rows": lax.rem(me + 1, n)},
        device_id_type=MESH,
    )
    to_prev = pltpu.make_async_remote_copy(
        src_ref=xraw.at[1],
        dst_ref=xraw.at[3],
        send_sem=halo_send.at[1],
        recv_sem=halo_recv.at[1],
        device_id={"rows": lax.rem(me + n - 1, n)},
        device_id_type=MESH,
    )

    @pl.when(jnp.logical_not(last))
    def _():
        to_next.start()

    @pl.when(jnp.logical_not(first))
    def _():
        to_prev.start()

    count1 = float(2 * n * width * (chans // GROUPS))
    scale1, bias1 = half_affine(
        gathered(slots1, 0), chans // GROUPS, count1, gain_in[...], shift_in[...]
    )

    row_in = lax.broadcasted_iota(jnp.int32, (width, chans), 0)
    tail_in = lax.broadcasted_iota(jnp.int32, (8, chans), 0)
    zeros_tail = jnp.zeros((pad - width, chans), BF16)

    def activate(i):
        y = silu_of_half(xraw[i].astype(F32) * scale1 + bias1)
        turned = pltpu.roll(y, 1, 0)
        xcat[i, 0:width, 0:chans] = jnp.where(row_in == 0, 0.0, turned).astype(BF16)
        end = jnp.where(tail_in == 0, turned[0:8], 0.0)
        end = jnp.concatenate([end, jnp.zeros((pad - width - 8, chans), F32)], axis=0)
        xcat[i, width:pad, 0:chans] = end.astype(BF16)
        xcat[i, 0:width, chans:] = y.astype(BF16)
        xcat[i, width:pad, chans:] = zeros_tail

    activate(1)
    activate(2)
    for c in loads:
        c.wait()

    def products(ks, bs):
        if ks:
            pairs = [jnp.concatenate([xcat[k], xcat[k + 1]], axis=1) for k in ks]
            res = dot(jnp.concatenate(pairs, axis=0), w1[0 : 4 * chans])
            for p, k in enumerate(ks):
                de[k] = res[p * pad : (p + 1) * pad]
            pairs = [
                jnp.concatenate([xcat[k, 0:width, chans:], xcat[k + 1, 0:width, chans:]], axis=1)
                for k in ks
            ]
            res = dot(jnp.concatenate(pairs, axis=0), w1[4 * chans : 6 * chans])
            for p, k in enumerate(ks):
                df[k] = res[p * width : (p + 1) * width]
        if bs:
            res = dot(jnp.concatenate([xcat[i] for i in bs], axis=0), w1[6 * chans : 8 * chans])
            for p, i in enumerate(bs):
                be[i] = res[p * pad : (p + 1) * pad]
            lhs = jnp.concatenate([xcat[i, 0:width, chans:] for i in bs], axis=0)
            res = dot(lhs, w1[8 * chans : 9 * chans])
            for p, i in enumerate(bs):
                bf[i] = res[p * width : (p + 1) * width]

    sums = [jnp.zeros((8, outs), F32), jnp.zeros((8, outs), F32)]

    def combine(r):
        k, i = r // 2, (r + 1) // 2
        edge = de[k] + be[i]
        whole = df[k] + bf[i]
        even = edge[0:width] + whole
        odd = pltpu.roll(edge, pad - 1, 0)[0:width] + whole
        hid[r, :, 0:outs] = even.astype(BF16)
        hid[r, :, outs:] = odd.astype(BF16)
        if 1 <= r <= 4:
            for v in (even, odd):
                v = v.reshape(width // 8, 8, outs)
                sums[0] = sums[0] + jnp.sum(v, axis=0)
                sums[1] = sums[1] + jnp.sum(v * v, axis=0)

    products((1,), (1, 2))
    combine(2)
    combine(3)

    @pl.when(jnp.logical_not(first))
    def _():
        to_next.wait_recv()
        activate(0)

    @pl.when(first)
    def _():
        xcat[0] = jnp.zeros(xcat.shape[1:], BF16)

    @pl.when(jnp.logical_not(last))
    def _():
        to_prev.wait_recv()
        activate(3)

    @pl.when(last)
    def _():
        xcat[3] = jnp.zeros(xcat.shape[1:], BF16)

    products((0, 2), ())
    for r in (1, 4):
        combine(r)

    total = jnp.sum(sums[0], axis=0, keepdims=True)
    square = jnp.sum(sums[1], axis=0, keepdims=True)
    lanes = outs // 128
    stat[1] = jnp.zeros(stat.shape[1:], F32)
    for k in range(lanes):
        stat[1, k : k + 1, :] = total[:, 128 * k : 128 * (k + 1)]
        stat[1, lanes + k : lanes + k + 1, :] = square[:, 128 * k : 128 * (k + 1)]
    exchange(slots2, 1)

    products((), (0, 3))
    for r in (0, 5):
        combine(r)
    load_ws.wait()
    for i in range(2):
        skip[i] = dot(xcat[1 + i, 0:width, chans:], ws[...])
    load_w2.wait()

    count2 = float(8 * n * width * (outs // GROUPS))
    scale2, bias2 = half_affine(
        gathered(slots2, 1), outs // GROUPS, count2, gain_mid[...], shift_mid[...]
    )
    row_mid = lax.broadcasted_iota(jnp.int32, (width, outs), 0)

    def middle(r):
        even = silu_of_half(hid[r, :, 0:outs].astype(F32) * scale2 + bias2)
        odd = silu_of_half(hid[r, :, outs:].astype(F32) * scale2 + bias2)
        if r == 0:
            even = jnp.where(first, 0.0, even)
            odd = jnp.where(first, 0.0, odd)
        if r == 5:
            even = jnp.where(last, 0.0, even)
            odd = jnp.where(last, 0.0, odd)
        before = jnp.where(row_mid == 0, 0.0, pltpu.roll(odd, 1, 0))
        after = jnp.where(row_mid == width - 1, 0.0, pltpu.roll(even, width - 1, 0))
        mid[r, :, 0:outs] = before.astype(BF16)
        mid[r, :, outs : 2 * outs] = even.astype(BF16)
        mid[r, :, 2 * outs : 3 * outs] = odd.astype(BF16)
        mid[r, :, 3 * outs :] = after.astype(BF16)

    def second(pair):
        rows = (2 * pair, 2 * pair + 1)
        base = jnp.concatenate([skip[pair], skip[pair]], axis=0)
        for parity in range(2):
            cols = pl.ds(parity * outs, 3 * outs)
            lhs = jnp.concatenate(
                [
                    jnp.concatenate([mid[r + a, :, cols] for a in range(3)], axis=1)
                    for r in rows
                ],
                axis=0,
            )
            res = dot(lhs, w2[...]) + base
            for h in range(outs // 128):
                inter[pair, h, pl.ds(parity, 2 * width, stride=2), :] = res[
                    :, 128 * h : 128 * (h + 1)
                ]
        for h in range(outs // 128):
            out[2 * pair : 2 * pair + 2, :, 128 * h : 128 * (h + 1)] = (
                inter[pair, h].astype(BF16).reshape(2, 2 * width, 128)
            )

    for r in range(4):
        middle(r)
    second(0)
    middle(4)
    middle(5)
    second(1)

    for index, slots in enumerate((slots1, slots2)):

        def sent(d, carry):
            peer_copy(slots, index, d).wait_send()
            return carry

        lax.fori_loop(1, n, sent, 0)

    @pl.when(jnp.logical_not(last))
    def _():
        to_next.wait_send()

    @pl.when(jnp.logical_not(first))
    def _():
        to_prev.wait_send()


def body(n, latent, gain_in, shift_in, conv_in, gain_mid, shift_mid, conv_mid, skip_weight):
    rows, width, chans = latent.shape
    outs = skip_weight.shape[1]
    pad = width + 16
    hbm = pl.BlockSpec(memory_space=pltpu.HBM)
    vmem = pl.BlockSpec(memory_space=pltpu.VMEM)
    return pl.pallas_call(
        functools.partial(kernel, n),
        out_shape=pltpu.VMEM((2 * rows, 2 * width, outs), BF16),
        in_specs=[hbm, vmem, vmem, hbm, vmem, vmem, hbm, hbm],
        out_specs=vmem,
        scratch_shapes=[
            pltpu.VMEM((4, width, chans), BF16),
            pltpu.VMEM((4, pad, 2 * chans), BF16),
            pltpu.VMEM((9 * chans, outs), BF16),
            pltpu.VMEM((9 * outs, outs), BF16),
            pltpu.VMEM((chans, outs), BF16),
            pltpu.VMEM((3, pad, outs), F32),
            pltpu.VMEM((4, pad, outs), F32),
            pltpu.VMEM((3, width, outs), F32),
            pltpu.VMEM((4, width, outs), F32),
            pltpu.VMEM((6, width, 2 * outs), BF16),
            pltpu.VMEM((6, width, 4 * outs), BF16),
            pltpu.VMEM((2, width, outs), F32),
            pltpu.VMEM((2, outs // 128, 4 * width, 128), F32),
            pltpu.VMEM((2, 8, 128), F32),
            pltpu.VMEM((n - 1, 8, 128), F32),
            pltpu.VMEM((n - 1, 8, 128), F32),
            pltpu.SemaphoreType.DMA((12,)),
            pltpu.SemaphoreType.DMA((2,)),
            pltpu.SemaphoreType.DMA((2,)),
            pltpu.SemaphoreType.DMA((2, n - 1)),
            pltpu.SemaphoreType.DMA((2, n - 1)),
        ],
        compiler_params=pltpu.CompilerParams(
            collective_id=0, has_side_effects=True, vmem_limit_bytes=56 * 1024 * 1024
        ),
        cost_estimate=pl.CostEstimate(
            flops=4_700_000_000, bytes_accessed=5_400_000, transcendentals=1_300_000
        ),
    )(
        latent,
        gain_in.reshape(1, chans),
        shift_in.reshape(1, chans),
        conv_in,
        gain_mid.reshape(1, outs),
        shift_mid.reshape(1, outs),
        conv_mid,
        skip_weight,
    )


def solution(mesh):
    placed = (P(("groups", "rows"), None, None), P(), P(), P(), P(), P(), P(), P())
    return jax.shard_map(
        functools.partial(body, mesh.shape["rows"]),
        mesh=mesh,
        in_specs=placed,
        out_specs=P(("groups", "rows"), None, None),
        check_vma=False,
    )
```
